256 devices in a mesh: dp: 16 (over y, x), shard: 16 (over z, core).
Axes of the slice: x: 4, y: 4, z: 8, core: 2. Of those that a mesh axis runs over, the one named last changes fastest.
Arguments:
- grad_parts: bfloat16 [16, 16, 1792, 1792], P('dp', None, 'shard'), may hold values from -5 to 5
- moment: bfloat16 [16, 1792, 1792], P('dp', 'shard'), may hold values from -6 to 6
- second: float32 [16, 1792, 1792], P('dp', 'shard'), may hold values from 0.1 to 10
- left_basis: bfloat16 [16, 1792, 1792], P('dp', 'shard'), may hold values from -0.125 to 0.125
- right_basis: bfloat16 [16, 1792, 1792], P('dp', 'shard'), may hold values from -0.125 to 0.125
- block_steps: int32 [16], P('dp'), may hold values from 1 to 40
Outputs:
- moment_new: bfloat16 [16, 1792, 1792], P('dp', 'shard')
- second_new: float32 [16, 1792, 1792], P('dp', 'shard')
- update: bfloat16 [16, 1792, 1792], P('dp', 'shard')
The draws below stay inside these ranges and needn't reach their ends.
All inputs are finite; a program needn't handle non-finite values.
Results may differ from the reference program's by a relative error of at most 0.017.
Values may be sent and summed in bfloat16 or wider, within the bound.
No kernel may reach another device: no remote copies, remote signals or barrier semaphores. Data moves between devices by JAX's collectives and lax.ppermute only.
A program may use at most 128 MiB of HBM per device.

```python
import math
import jax
import jax.numpy as jnp
from jax import lax

BS = 1792
NB = 16
N_DP = 16


def plant(values, own_key, smallest, top_value):
    longest = values.shape.index(max(values.shape))
    spots = []
    for shift in (0, 1):
        where = [jax.random.randint(jax.random.fold_in(own_key, axis), (), 0, length) for axis, length in enumerate(values.shape)]
        where[longest] = (where[longest] + shift) % values.shape[longest]
        spots.append(tuple(where))
    return values.at[spots[0]].set(smallest).at[spots[1]].set(top_value)


def with_spikes(drawn, rng, source, target, blocks, factor):
    owner, partner = [(jnp.arange(drawn.shape[position]) // (drawn.shape[position] // blocks)).reshape([-1 if axis == position else 1 for axis in range(drawn.ndim)]) for position in (source, target)]
    chosen = jax.random.permutation(rng, blocks)[partner]
    strong = (owner == chosen) | (owner == (partner + blocks // 2) % blocks)
    return jnp.where(strong, factor * drawn, drawn)


def block_levels(stream_key, extent, cuts, low, high):
    def one(position, shards_of):
        draws = jax.random.uniform(jax.random.fold_in(jax.random.fold_in(stream_key, 6), position), (shards_of,), jnp.float32, low / len(cuts), high / len(cuts))
        return jnp.repeat(jnp.exp(draws), extent[position] // shards_of).reshape((-1,) + (1,) * (len(extent) - position - 1))

    factor_of = one(*cuts[0])
    for cut in cuts[1:]:
        factor_of = factor_of * one(*cut)
    return factor_of


def gaussian(rng, dims, deviation, bound, split=(), held_as=jnp.bfloat16):
    values = deviation * jax.random.normal(rng, dims, jnp.float32)
    if split:
        values = values * block_levels(rng, dims, split, -0.22, 0.18)
    return jnp.clip(values, -bound, bound).astype(held_as)


def heavy_noise(rng, extent, spread, reach, pieces, heavy, kind=jnp.bfloat16):
    result = spread * jax.random.normal(rng, extent, jnp.float32)
    if pieces:
        result = result * block_levels(rng, extent, pieces, -0.22, 0.18)
    return jnp.clip(with_spikes(result, jax.random.fold_in(rng, 3), *heavy), -reach, reach).astype(kind)


def setup_inputs(seed: int = 0) -> dict:
    seeds = jax.random.split(jax.random.key(seed), 7)
    return {
        "grad_parts": heavy_noise(seeds[0], (N_DP, NB, BS, BS), 0.25, 5.0, ((0, 16), (2, 16)), (0, 1, 16, 2.0)),
        "moment": gaussian(seeds[1], (NB, BS, BS), 1.0, 6.0, ((0, 16), (1, 16))),
        "second": jnp.clip(jnp.exp(math.log(10.0) - 4.6051702 * jax.random.uniform(seeds[2], (NB, BS, BS), jnp.float32) ** block_levels(seeds[2], (NB, BS, BS), ((0, 16), (1, 16)), -0.2, 0.2)), 0.1, 10.0),
        "left_basis": gaussian(seeds[3], (NB, BS, BS), BS ** -0.5, 0.125, ((0, 16), (1, 16))),
        "right_basis": gaussian(seeds[4], (NB, BS, BS), BS ** -0.5, 0.125, ((0, 16), (1, 16))),
        "block_steps": plant(jax.random.randint(seeds[5], (NB,), 1, 41), jax.random.fold_in(seeds[5], 1), 1, 40).astype(jnp.int32),
    }


beta_one = 0.8
beta_two = 0.95
epsilon = 1e-08

def rotate_block(operands):
    gradient, moment_new, second, left_basis, right_basis, count = operands
    left_grad = jnp.dot(left_basis.T, gradient, preferred_element_type=jnp.float32).astype(jnp.bfloat16)
    left_mom = jnp.dot(left_basis.T, moment_new, preferred_element_type=jnp.float32).astype(jnp.bfloat16)
    rot_grad = jnp.dot(left_grad, right_basis, preferred_element_type=jnp.float32)
    rot_mom = jnp.dot(left_mom, right_basis, preferred_element_type=jnp.float32)
    second_new = beta_two * second + (1.0 - beta_two) * rot_grad * rot_grad
    steps_float = count.astype(jnp.float32)
    first_fix = 1.0 - jnp.power(jnp.float32(beta_one), steps_float)
    second_fix = 1.0 - jnp.power(jnp.float32(beta_two), steps_float)
    direction = (rot_mom / first_fix / (jnp.sqrt(second_new / second_fix) + epsilon)).astype(jnp.bfloat16)
    back = jnp.dot(direction, right_basis.T, preferred_element_type=jnp.float32).astype(jnp.bfloat16)
    update = jnp.dot(left_basis, back, preferred_element_type=jnp.float32).astype(jnp.bfloat16)
    return (second_new, update)

def reference(grad_parts, moment, second, left_basis, right_basis, block_steps):

    def add_part(index, running):
        return running + grad_parts[index].astype(jnp.float32)
    summed = lax.fori_loop(0, grad_parts.shape[0], add_part, jnp.zeros(grad_parts.shape[1:], jnp.float32))
    gradient = summed.astype(jnp.bfloat16)
    moment_new = (beta_one * moment.astype(jnp.float32) + (1.0 - beta_one) * gradient.astype(jnp.float32)).astype(jnp.bfloat16)
    second_new, update = lax.map(rotate_block, (gradient, moment_new, second, left_basis, right_basis, block_steps))
    return (moment_new, second_new, update)
```

```python
import jax
import jax.numpy as jnp
from jax import lax
from jax.sharding import PartitionSpec as P

beta_one = 0.8
beta_two = 0.95
epsilon = 1e-08
f32, bf16 = jnp.float32, jnp.bfloat16
SIDE = 4
TOGETHER = 56


def swaps(axis, mask):
    if axis:
        return [(y * SIDE + x, y * SIDE + (x ^ mask)) for y in range(SIDE) for x in range(SIDE)]
    return [(y * SIDE + x, (y ^ mask) * SIDE + x) for y in range(SIDE) for x in range(SIDE)]


def halving(values, at, order):
    spot = list(at)
    for axis in order:

        def own(mask, axis=axis, values=values):
            return lax.dynamic_index_in_dim(values, spot[axis] ^ mask, axis=axis, keepdims=True).astype(f32)

        away = jnp.concatenate([own(1), own(2)], axis=axis).astype(bf16)
        got = lax.ppermute(away, "dp", swaps(axis, 1)).astype(f32)
        first, second = jnp.split(got, 2, axis=axis)
        across = lax.ppermute((own(3) + second).astype(bf16), "dp", swaps(axis, 3))
        values = own(0) + first + across.astype(f32)
        spot[axis] = 0
    return values[0, 0]


def reduce_blocks(parts):
    rows, columns = parts.shape[1:]
    me = lax.axis_index("dp")
    at = (me // SIDE, me % SIDE)
    upper = lax.psum_scatter(parts[:, :TOGETHER], "dp", scatter_dimension=0, tiled=True)[0]
    grid = parts.reshape(SIDE, SIDE, rows, columns)[:, :, TOGETHER:]
    left = halving(grid[..., : columns // 2], at, (1, 0))
    right = halving(grid[..., columns // 2 :], at, (0, 1))
    lower = jnp.concatenate([left, right], axis=1).astype(bf16)
    return jnp.concatenate([upper, lower], axis=0)


def to_cols(rows):
    return lax.all_to_all(rows, "shard", split_axis=rows.ndim - 1, concat_axis=rows.ndim - 2, tiled=True)


def to_rows(cols):
    return lax.all_to_all(cols, "shard", split_axis=cols.ndim - 2, concat_axis=cols.ndim - 1, tiled=True)


def local(grad_parts, moment, second, left_basis, right_basis, block_steps):
    right_full = lax.all_gather(right_basis[0], "shard", axis=0, tiled=True)
    left_full = lax.all_gather(left_basis[0], "shard", axis=0, tiled=True)
    gradient = reduce_blocks(grad_parts[0])
    second_cols = to_cols(second[0].astype(bf16))
    gradient, second_cols = lax.optimization_barrier((gradient, second_cols))
    moment_new = (beta_one * moment[0].astype(f32) + (1.0 - beta_one) * gradient.astype(f32)).astype(bf16)

    pair = jnp.stack([gradient, moment_new])
    pair_right = jnp.einsum("nrk,kc->nrc", pair, right_full, preferred_element_type=f32).astype(bf16)
    pair_cols = to_cols(pair_right)
    rot_grad, rot_mom = jnp.einsum("ki,nkc->nic", left_full, pair_cols, preferred_element_type=f32)

    second_new_cols = beta_two * second_cols.astype(f32) + (1.0 - beta_two) * rot_grad * rot_grad
    steps_float = block_steps[0].astype(f32)
    first_fix = 1.0 - jnp.power(f32(beta_one), steps_float)
    second_fix = 1.0 - jnp.power(f32(beta_two), steps_float)
    direction = (rot_mom / first_fix / (jnp.sqrt(second_new_cols / second_fix) + epsilon)).astype(bf16)
    left_dir = jnp.dot(left_full, direction, preferred_element_type=f32).astype(bf16)

    rot_grad_rows, left_dir_rows = to_rows(jnp.stack([rot_grad.astype(bf16), left_dir]))
    rot_grad_rows = rot_grad_rows.astype(f32)
    second_new = beta_two * second[0] + (1.0 - beta_two) * rot_grad_rows * rot_grad_rows
    update = jnp.einsum("rc,kc->rk", left_dir_rows, right_full, preferred_element_type=f32).astype(bf16)
    return (moment_new[None], second_new[None], update[None])


def solution(mesh):
    return jax.shard_map(
        local,
        mesh=mesh,
        in_specs=(
            P("dp", None, "shard", None),
            P("dp", "shard", None),
            P("dp", "shard", None),
            P("dp", "shard", None),
            P("dp", "shard", None),
            P("dp"),
        ),
        out_specs=(P("dp", "shard", None), P("dp", "shard", None), P("dp", "shard", None)),
        check_vma=False,
    )
```

```python
import jax
import jax.numpy as jnp
from jax import lax
from jax.sharding import PartitionSpec as P

beta_one = 0.8
beta_two = 0.95
epsilon = 1e-08
f32, bf16 = jnp.float32, jnp.bfloat16
SIDE = 4


def swaps(axis, mask):
    if axis:
        return [(y * SIDE + x, y * SIDE + (x ^ mask)) for y in range(SIDE) for x in range(SIDE)]
    return [(y * SIDE + x, (y ^ mask) * SIDE + x) for y in range(SIDE) for x in range(SIDE)]


def halving(grid, corner, extent, at, order, mask):
    other = mask ^ 2
    spot = list(at)
    for axis in order:

        def own(flip, axis=axis, grid=grid, corner=corner):
            start = [0, 0, *corner]
            start[axis] = spot[axis] ^ flip
            sizes = [*grid.shape[:2], *extent]
            sizes[axis] = 1
            return lax.dynamic_slice(grid, start, sizes)

        away = jnp.concatenate([own(mask), own(2)], axis=axis).astype(bf16)
        got = lax.ppermute(away, "dp", swaps(axis, mask))
        first = lax.slice_in_dim(got, 0, 1, axis=axis).astype(f32)
        second = lax.slice_in_dim(got, 1, 2, axis=axis).astype(f32)
        across = (own(other).astype(f32) + second).astype(bf16)
        across = lax.ppermute(across, "dp", swaps(axis, other))
        grid = own(0).astype(f32) + first + across.astype(f32)
        spot[axis], corner = 0, (0, 0)
    return grid[0, 0]


def reduce_blocks(parts):
    rows, columns = parts.shape[1:]
    me = lax.axis_index("dp")
    at = (me // SIDE, me % SIDE)
    grid = parts.reshape(SIDE, SIDE, rows, columns)
    extent = (rows // 2, columns // 2)
    streams = [((1, 0), 1), ((0, 1), 1), ((1, 0), 3), ((0, 1), 3)]
    quarters = [
        halving(grid, (r * extent[0], c * extent[1]), extent, at, *streams[2 * r + c]) for r in range(2) for c in range(2)
    ]
    upper, lower = jnp.concatenate(quarters[:2], axis=1), jnp.concatenate(quarters[2:], axis=1)
    return jnp.concatenate([upper, lower], axis=0).astype(bf16)


def to_cols(rows):
    return lax.all_to_all(rows, "shard", split_axis=rows.ndim - 1, concat_axis=rows.ndim - 2, tiled=True)


def to_rows(cols):
    return lax.all_to_all(cols, "shard", split_axis=cols.ndim - 2, concat_axis=cols.ndim - 1, tiled=True)


def local(grad_parts, moment, second, left_basis, right_basis, block_steps):
    right_full = lax.all_gather(right_basis[0], "shard", axis=0, tiled=True)
    left_full = lax.all_gather(left_basis[0], "shard", axis=0, tiled=True)
    gradient = reduce_blocks(grad_parts[0])
    second_cols = to_cols(second[0].astype(bf16))
    gradient, second_cols = lax.optimization_barrier((gradient, second_cols))
    moment_new = (beta_one * moment[0].astype(f32) + (1.0 - beta_one) * gradient.astype(f32)).astype(bf16)

    pair = jnp.stack([gradient, moment_new])
    pair_right = jnp.einsum("nrk,kc->nrc", pair, right_full, preferred_element_type=f32).astype(bf16)
    pair_cols = to_cols(pair_right)
    rot_grad, rot_mom = jnp.einsum("ki,nkc->nic", left_full, pair_cols, preferred_element_type=f32)

    second_new_cols = beta_two * second_cols.astype(f32) + (1.0 - beta_two) * rot_grad * rot_grad
    steps_float = block_steps[0].astype(f32)
    first_fix = 1.0 - jnp.power(f32(beta_one), steps_float)
    second_fix = 1.0 - jnp.power(f32(beta_two), steps_float)
    direction = (rot_mom / first_fix / (jnp.sqrt(second_new_cols / second_fix) + epsilon)).astype(bf16)
    left_dir = jnp.dot(left_full, direction, preferred_element_type=f32).astype(bf16)

    rot_grad_rows, left_dir_rows = to_rows(jnp.stack([rot_grad.astype(bf16), left_dir]))
    rot_grad_rows = rot_grad_rows.astype(f32)
    second_new = beta_two * second[0] + (1.0 - beta_two) * rot_grad_rows * rot_grad_rows
    update = jnp.einsum("rc,kc->rk", left_dir_rows, right_full, preferred_element_type=f32).astype(bf16)
    return (moment_new[None], second_new[None], update[None])


def solution(mesh):
    return jax.shard_map(
        local,
        mesh=mesh,
        in_specs=(
            P("dp", None, "shard", None),
            P("dp", "shard", None),
            P("dp", "shard", None),
            P("dp", "shard", None),
            P("dp", "shard", None),
            P("dp"),
        ),
        out_specs=(P("dp", "shard", None), P("dp", "shard", None), P("dp", "shard", None)),
        check_vma=False,
    )
```

```python
import jax
import jax.numpy as jnp
from jax import lax
from jax.sharding import PartitionSpec as P

beta_one = 0.8
beta_two = 0.95
epsilon = 1e-08
f32, bf16 = jnp.float32, jnp.bfloat16


def to_cols(rows):
    return lax.all_to_all(rows, "shard", split_axis=rows.ndim - 1, concat_axis=rows.ndim - 2, tiled=True)


def to_rows(cols):
    return lax.all_to_all(cols, "shard", split_axis=cols.ndim - 2, concat_axis=cols.ndim - 1, tiled=True)


def local(grad_parts, moment, second, left_basis, right_basis, block_steps):
    gradient = lax.psum_scatter(grad_parts[0], "dp", scatter_dimension=0, tiled=True)[0]
    bases = jnp.concatenate([right_basis, left_basis], axis=0)
    right_full, left_full = lax.all_gather(bases, "shard", axis=1, tiled=True)
    second_cols = to_cols(second[0].astype(bf16))
    gradient, second_cols = lax.optimization_barrier((gradient, second_cols))

    moment_new = (beta_one * moment[0].astype(f32) + (1.0 - beta_one) * gradient.astype(f32)).astype(bf16)
    pair = jnp.stack([gradient, moment_new])
    pair_right = jnp.einsum("nrk,kc->nrc", pair, right_full, preferred_element_type=f32).astype(bf16)
    pair_cols = to_cols(pair_right)
    rot_grad, rot_mom = jnp.einsum("ki,nkc->nic", left_full, pair_cols, preferred_element_type=f32)

    second_new_cols = beta_two * second_cols.astype(f32) + (1.0 - beta_two) * rot_grad * rot_grad
    steps_float = block_steps[0].astype(f32)
    first_fix = 1.0 - jnp.power(f32(beta_one), steps_float)
    second_fix = 1.0 - jnp.power(f32(beta_two), steps_float)
    direction = (rot_mom / first_fix / (jnp.sqrt(second_new_cols / second_fix) + epsilon)).astype(bf16)
    left_dir = jnp.dot(left_full, direction, preferred_element_type=f32).astype(bf16)

    rot_grad_rows, left_dir_rows = to_rows(jnp.stack([rot_grad.astype(bf16), left_dir]))
    rot_grad_rows = rot_grad_rows.astype(f32)
    second_new = beta_two * second[0] + (1.0 - beta_two) * rot_grad_rows * rot_grad_rows
    update = jnp.einsum("rc,kc->rk", left_dir_rows, right_full, preferred_element_type=f32).astype(bf16)
    return (moment_new[None], second_new[None], update[None])


def solution(mesh):
    return jax.shard_map(
        local,
        mesh=mesh,
        in_specs=(
            P("dp", None, "shard", None),
            P("dp", "shard", None),
            P("dp", "shard", None),
            P("dp", "shard", None),
            P("dp", "shard", None),
            P("dp"),
        ),
        out_specs=(P("dp", "shard", None), P("dp", "shard", None), P("dp", "shard", None)),
        check_vma=False,
    )
```

```python
import jax
import jax.numpy as jnp
from jax import lax
from jax.sharding import PartitionSpec as P

beta_one = 0.8
beta_two = 0.95
epsilon = 1e-08
f32, bf16 = jnp.float32, jnp.bfloat16


def to_cols(rows):
    return lax.all_to_all(rows, "shard", split_axis=rows.ndim - 1, concat_axis=rows.ndim - 2, tiled=True)


def to_rows(cols):
    return lax.all_to_all(cols, "shard", split_axis=cols.ndim - 2, concat_axis=cols.ndim - 1, tiled=True)


def local(grad_parts, moment, second, left_basis, right_basis, block_steps):
    gradient = lax.psum_scatter(grad_parts[0], "dp", scatter_dimension=0, tiled=True)[0]
    right_full = lax.all_gather(right_basis[0], "shard", axis=0, tiled=True)
    left_full = lax.all_gather(left_basis[0], "shard", axis=0, tiled=True)
    second_cols = to_cols(second[0].astype(bf16))
    mom_right = jnp.dot(moment[0], right_full, preferred_element_type=f32).astype(bf16)
    mom_cols = to_cols(mom_right)
    gradient, second_cols, mom_cols = lax.optimization_barrier((gradient, second_cols, mom_cols))

    moment_new = (beta_one * moment[0].astype(f32) + (1.0 - beta_one) * gradient.astype(f32)).astype(bf16)
    grad_right = jnp.dot(gradient, right_full, preferred_element_type=f32).astype(bf16)
    grad_cols = to_cols(grad_right)
    pair_cols = jnp.stack([grad_cols, mom_cols])
    rot_grad, rot_mom_old = jnp.einsum("ki,nkc->nic", left_full, pair_cols, preferred_element_type=f32)
    rot_mom = beta_one * rot_mom_old + (1.0 - beta_one) * rot_grad

    second_new_cols = beta_two * second_cols.astype(f32) + (1.0 - beta_two) * rot_grad * rot_grad
    steps_float = block_steps[0].astype(f32)
    first_fix = 1.0 - jnp.power(f32(beta_one), steps_float)
    second_fix = 1.0 - jnp.power(f32(beta_two), steps_float)
    direction = (rot_mom / first_fix / (jnp.sqrt(second_new_cols / second_fix) + epsilon)).astype(bf16)
    left_dir = jnp.dot(left_full, direction, preferred_element_type=f32).astype(bf16)

    rot_grad_rows, left_dir_rows = to_rows(jnp.stack([rot_grad.astype(bf16), left_dir]))
    rot_grad_rows = rot_grad_rows.astype(f32)
    second_new = beta_two * second[0] + (1.0 - beta_two) * rot_grad_rows * rot_grad_rows
    update = jnp.einsum("rc,kc->rk", left_dir_rows, right_full, preferred_element_type=f32).astype(bf16)
    return (moment_new[None], second_new[None], update[None])


def solution(mesh):
    return jax.shard_map(
        local,
        mesh=mesh,
        in_specs=(
            P("dp", None, "shard", None),
            P("dp", "shard", None),
            P("dp", "shard", None),
            P("dp", "shard", None),
            P("dp", "shard", None),
            P("dp"),
        ),
        out_specs=(P("dp", "shard", None), P("dp", "shard", None), P("dp", "shard", None)),
        check_vma=False,
    )
```

```python
import jax
import jax.numpy as jnp
from jax import lax
from jax.experimental import pallas as pl
from jax.experimental.pallas import tpu as pltpu
from jax.sharding import PartitionSpec as P

beta_one = 0.8
beta_two = 0.95
epsilon = 1e-08
f32, bf16 = jnp.float32, jnp.bfloat16
GROUP = 16
TILE = 256
VMEM_LIMIT = 48 * 2**20
by_rows = (((1,), (1,)), ((), ()))


def whole():
    return pl.BlockSpec(memory_space=pltpu.VMEM)


def spread(x_ref, out_ref, *lead):
    width = out_ref.shape[-1]
    for s in range(GROUP):
        out_ref[(s, *lead)] = x_ref[:, s * width : (s + 1) * width].astype(out_ref.dtype)


def cut_kernel(x_ref, out_ref):
    spread(x_ref, out_ref)


def right_kernel(a_ref, right_ref, out_ref, x_ref):
    @pl.loop(0, x_ref.shape[1] // TILE)
    def _(t):
        tile = pl.ds(pl.multiple_of(t * TILE, TILE), TILE)
        x_ref[:, tile] = jnp.dot(a_ref[...], right_ref[:, tile], preferred_element_type=f32)

    spread(x_ref, out_ref)


def middle_kernel(fix_ref, grad_ref, mom_ref, second_ref, left_ref, out_ref, pair_ref, second_t, rot_ref, dir_ref, back_ref):
    width = grad_ref.shape[1]
    pair_ref[:width] = grad_ref[...].astype(f32).T.astype(bf16)
    pair_ref[width:] = mom_ref[...].astype(f32).T.astype(bf16)
    second_t[...] = second_ref[...].astype(f32).T

    @pl.loop(0, rot_ref.shape[1] // TILE)
    def _(t):
        tile = pl.ds(pl.multiple_of(t * TILE, TILE), TILE)
        both = jnp.dot(pair_ref[...], left_ref[:, tile], preferred_element_type=f32)
        rot_grad = both[:width]
        rot_mom = beta_one * both[width:] + (1.0 - beta_one) * rot_grad
        rot_ref[:, tile] = rot_grad
        second_new = beta_two * second_t[:, tile] + (1.0 - beta_two) * rot_grad * rot_grad
        direction = rot_mom / fix_ref[0] / (jnp.sqrt(second_new / fix_ref[1]) + epsilon)
        dir_ref[:, tile] = direction.astype(bf16)

    @pl.loop(0, rot_ref.shape[1] // TILE)
    def _(t):
        tile = pl.ds(pl.multiple_of(t * TILE, TILE), TILE)
        back_ref[:, tile] = lax.dot_general(dir_ref[...], left_ref[tile, :], by_rows, preferred_element_type=f32)

    spread(rot_ref, out_ref, 0)
    spread(back_ref, out_ref, 1)


def last_kernel(in_ref, second_ref, right_ref, second_out, update_out, rows_ref):
    columns = second_ref.shape[1]
    width = in_ref.shape[-1]
    rot_grad = in_ref[:, 0].reshape(columns, width).astype(f32).T
    second_out[...] = beta_two * second_ref[...] + (1.0 - beta_two) * rot_grad * rot_grad
    rows_ref[...] = in_ref[:, 1].reshape(columns, width).astype(f32).T.astype(bf16)

    @pl.loop(0, columns // TILE)
    def _(t):
        tile = pl.ds(pl.multiple_of(t * TILE, TILE), TILE)
        update_out[:, tile] = lax.dot_general(rows_ref[...], right_ref[tile, :], by_rows, preferred_element_type=f32).astype(bf16)


def call(kernel, out_shape, in_specs, scratch, flops, moved):
    return pl.pallas_call(
        kernel,
        out_shape=out_shape,
        in_specs=in_specs,
        out_specs=jax.tree.map(lambda _: whole(), out_shape),
        scratch_shapes=scratch,
        compiler_params=pltpu.CompilerParams(vmem_limit_bytes=VMEM_LIMIT),
        cost_estimate=pl.CostEstimate(flops=flops, bytes_accessed=moved, transcendentals=0),
    )


def swap(pieces):
    return lax.all_to_all(pieces, "shard", split_axis=0, concat_axis=0, tiled=True)


def local(grad_parts, moment, second, left_basis, right_basis, block_steps):
    rows, columns = moment.shape[1:]
    product = 2 * rows * columns * columns
    basis_bytes = 2 * columns * columns
    pieces = jax.ShapeDtypeStruct((GROUP, rows, rows), bf16)
    times_right = call(right_kernel, pieces, [whole()] * 2, [pltpu.VMEM((rows, columns), f32)], product, basis_bytes)

    gradient = lax.psum_scatter(grad_parts[0], "dp", scatter_dimension=0, tiled=True)[0]
    right_full = lax.all_gather(right_basis[0], "shard", axis=0, tiled=True)
    left_full = lax.all_gather(left_basis[0], "shard", axis=0, tiled=True)
    second_cols = swap(call(cut_kernel, pieces, [whole()], [], 0, 6 * rows * columns)(second[0]))
    mom_cols = swap(times_right(moment[0], right_full))
    gradient, second_cols, mom_cols = lax.optimization_barrier((gradient, second_cols, mom_cols))

    moment_new = (beta_one * moment[0].astype(f32) + (1.0 - beta_one) * gradient.astype(f32)).astype(bf16)
    grad_cols = swap(times_right(gradient, right_full))

    steps_float = block_steps[0].astype(f32)
    fixes = jnp.stack([1.0 - jnp.power(f32(beta_one), steps_float), 1.0 - jnp.power(f32(beta_two), steps_float)])
    flat = [cols.reshape(columns, rows) for cols in (grad_cols, mom_cols, second_cols)]
    scratch = [
        pltpu.VMEM((2 * rows, columns), bf16),
        pltpu.VMEM((rows, columns), f32),
        pltpu.VMEM((rows, columns), f32),
        pltpu.VMEM((rows, columns), bf16),
        pltpu.VMEM((rows, columns), f32),
    ]
    both = jax.ShapeDtypeStruct((GROUP, 2, rows, rows), bf16)
    specs = [pl.BlockSpec(memory_space=pltpu.SMEM)] + [whole()] * 4
    sent = call(middle_kernel, both, specs, scratch, 3 * product, basis_bytes)(fixes, *flat, left_full)

    got = swap(sent)
    outs = (jax.ShapeDtypeStruct((rows, columns), f32), jax.ShapeDtypeStruct((rows, columns), bf16))
    scratch = [pltpu.VMEM((rows, columns), bf16)]
    second_new, update = call(last_kernel, outs, [whole()] * 3, scratch, product, basis_bytes)(got, second[0], right_full)
    return (moment_new[None], second_new[None], update[None])


def solution(mesh):
    return jax.shard_map(
        local,
        mesh=mesh,
        in_specs=(
            P("dp", None, "shard", None),
            P("dp", "shard", None),
            P("dp", "shard", None),
            P("dp", "shard", None),
            P("dp", "shard", None),
            P("dp"),
        ),
        out_specs=(P("dp", "shard", None), P("dp", "shard", None), P("dp", "shard", None)),
        check_vma=False,
    )
```

```python
import jax
import jax.numpy as jnp
from jax import lax
from jax.experimental import pallas as pl
from jax.experimental.pallas import tpu as pltpu
from jax.sharding import PartitionSpec as P

beta_one = 0.8
beta_two = 0.95
epsilon = 1e-08
f32, bf16 = jnp.float32, jnp.bfloat16
GROUP = 16
TILE = 256
VMEM_LIMIT = 48 * 2**20
by_rows = (((1,), (1,)), ((), ()))


def whole():
    return pl.BlockSpec(memory_space=pltpu.VMEM)


def spread(x_ref, out_ref, *lead):
    width = out_ref.shape[-1]
    for s in range(GROUP):
        out_ref[(s, *lead)] = x_ref[:, s * width : (s + 1) * width].astype(out_ref.dtype)


def fetch(basis_ref, held, sems, by_column):
    copies = []
    for t in range(basis_ref.shape[0] // TILE):
        tile = pl.ds(t * TILE, TILE)
        spot = (slice(None), tile) if by_column else (tile, slice(None))
        copies.append(pltpu.make_async_copy(basis_ref.at[spot], held.at[spot], sems.at[t]))
        copies[-1].start()
    return copies


def cut_kernel(x_ref, out_ref):
    spread(x_ref, out_ref)


def turn_kernel(x_ref, out_ref):
    out_ref[...] = x_ref[...].astype(f32).T.astype(bf16)


def right_kernel(a_ref, right_ref, out_ref, x_ref, held, sems):
    for t, copy in enumerate(fetch(right_ref, held, sems, True)):
        copy.wait()
        tile = slice(t * TILE, (t + 1) * TILE)
        x_ref[:, tile] = jnp.dot(a_ref[...], held[:, tile], preferred_element_type=f32)
    spread(x_ref, out_ref)


def moment_kernel(cols_ref, left_ref, out_ref, held, sems):
    copies = fetch(left_ref, held, sems, True)
    x = cols_ref[...].astype(f32).T.astype(bf16)
    for t, copy in enumerate(copies):
        copy.wait()
        tile = slice(t * TILE, (t + 1) * TILE)
        out_ref[:, tile] = jnp.dot(x, held[:, tile], preferred_element_type=f32)


def middle_kernel(fix_ref, cols_ref, mom_ref, second_ref, left_ref, out_ref, rot_ref, dir_ref, back_ref, held, sems):
    copies = fetch(left_ref, held, sems, True)
    x = cols_ref[...].astype(f32).T.astype(bf16)
    for t, copy in enumerate(copies):
        copy.wait()
        tile = slice(t * TILE, (t + 1) * TILE)
        rot_grad = jnp.dot(x, held[:, tile], preferred_element_type=f32)
        rot_ref[:, tile] = rot_grad
        rot_mom = beta_one * mom_ref[:, tile] + (1.0 - beta_one) * rot_grad
        second_new = beta_two * second_ref[:, tile].astype(f32) + (1.0 - beta_two) * rot_grad * rot_grad
        direction = rot_mom * fix_ref[0] / (jnp.sqrt(second_new * fix_ref[1]) + epsilon)
        dir_ref[:, tile] = direction.astype(bf16)
    spread(rot_ref, out_ref, 0)
    for t in range(len(copies)):
        tile = slice(t * TILE, (t + 1) * TILE)
        back_ref[:, tile] = lax.dot_general(dir_ref[...], held[tile, :], by_rows, preferred_element_type=f32)
    spread(back_ref, out_ref, 1)


def last_kernel(in_ref, second_ref, right_ref, second_out, update_out, held, sems):
    copies = fetch(right_ref, held, sems, False)
    columns = second_ref.shape[1]
    width = in_ref.shape[-1]
    rows = in_ref[:, 1].reshape(columns, width).astype(f32).T.astype(bf16)
    for t, copy in enumerate(copies):
        copy.wait()
        tile = slice(t * TILE, (t + 1) * TILE)
        update_out[:, tile] = lax.dot_general(rows, held[tile, :], by_rows, preferred_element_type=f32).astype(bf16)
    rot_grad = in_ref[:, 0].reshape(columns, width).astype(f32).T
    second_out[...] = beta_two * second_ref[...] + (1.0 - beta_two) * rot_grad * rot_grad


def call(kernel, out_shape, in_specs, scratch, flops, moved):
    return pl.pallas_call(
        kernel,
        out_shape=out_shape,
        in_specs=in_specs,
        out_specs=jax.tree.map(lambda _: whole(), out_shape),
        scratch_shapes=scratch,
        compiler_params=pltpu.CompilerParams(vmem_limit_bytes=VMEM_LIMIT),
        cost_estimate=pl.CostEstimate(flops=flops, bytes_accessed=moved, transcendentals=0),
    )


def swap(pieces):
    return lax.all_to_all(pieces, "shard", split_axis=0, concat_axis=0, tiled=True)


def local(grad_parts, moment, second, left_basis, right_basis, block_steps):
    rows, columns = moment.shape[1:]
    product = 2 * rows * columns * columns
    basis_bytes = 2 * columns * columns
    apart = pl.BlockSpec(memory_space=pl.ANY)
    narrow = pltpu.VMEM((rows, columns), bf16)
    wide = pltpu.VMEM((rows, columns), f32)
    basis = [pltpu.VMEM((columns, columns), bf16), pltpu.SemaphoreType.DMA((columns // TILE,))]
    pieces = jax.ShapeDtypeStruct((GROUP, rows, rows), bf16)
    turned = jax.ShapeDtypeStruct((rows, columns), bf16)
    summed = jax.ShapeDtypeStruct((rows, columns), f32)
    times_right = call(right_kernel, pieces, [whole(), apart], [wide, *basis], product, basis_bytes)

    gradient = lax.psum_scatter(grad_parts[0], "dp", scatter_dimension=0, tiled=True)[0]
    right_full = lax.all_gather(right_basis[0], "shard", axis=0, tiled=True)
    left_full = lax.all_gather(left_basis[0], "shard", axis=0, tiled=True)
    second_cols = swap(call(cut_kernel, pieces, [whole()], [], 0, 6 * rows * columns)(second[0]))
    second_turned = call(turn_kernel, turned, [whole()], [], 0, 4 * rows * columns)(second_cols.reshape(columns, rows))
    mom_cols = swap(times_right(moment[0], right_full))
    gradient, second_turned, mom_cols = lax.optimization_barrier((gradient, second_turned, mom_cols))

    moment_new = (beta_one * moment[0].astype(f32) + (1.0 - beta_one) * gradient.astype(f32)).astype(bf16)
    grad_cols = swap(times_right(gradient, right_full))
    times_left = call(moment_kernel, summed, [whole(), apart], basis, product, basis_bytes)
    rot_mom_old = times_left(mom_cols.reshape(columns, rows), left_full)

    steps_float = block_steps[0].astype(f32)
    fixes = 1.0 / jnp.stack([1.0 - jnp.power(f32(beta_one), steps_float), 1.0 - jnp.power(f32(beta_two), steps_float)])
    both = jax.ShapeDtypeStruct((GROUP, 2, rows, rows), bf16)
    specs = [pl.BlockSpec(memory_space=pltpu.SMEM), whole(), whole(), whole(), apart]
    middle = call(middle_kernel, both, specs, [wide, narrow, wide, *basis], 2 * product, basis_bytes)
    sent = middle(fixes, grad_cols.reshape(columns, rows), rot_mom_old, second_turned, left_full)

    got = swap(sent)
    last = call(last_kernel, (summed, turned), [whole(), whole(), apart], basis, product, basis_bytes)
    second_new, update = last(got, second[0], right_full)
    return (moment_new[None], second_new[None], update[None])


def solution(mesh):
    return jax.shard_map(
        local,
        mesh=mesh,
        in_specs=(
            P("dp", None, "shard", None),
            P("dp", "shard", None),
            P("dp", "shard", None),
            P("dp", "shard", None),
            P("dp", "shard", None),
            P("dp"),
        ),
        out_specs=(P("dp", "shard", None), P("dp", "shard", None), P("dp", "shard", None)),
        check_vma=False,
    )
```

```python
import jax
import jax.numpy as jnp
from jax import lax
from jax.experimental import pallas as pl
from jax.experimental.pallas import tpu as pltpu
from jax.sharding import PartitionSpec as P

beta_one = 0.8
beta_two = 0.95
epsilon = 1e-08
f32, bf16 = jnp.float32, jnp.bfloat16
GROUP = 16
TILE = 256
VMEM_LIMIT = 14 * 2**20
by_rows = (((1,), (1,)), ((), ()))


def whole():
    return pl.BlockSpec(memory_space=pltpu.VMEM)


def spread(x_ref, out_ref, *lead):
    width = out_ref.shape[-1]
    for s in range(GROUP):
        out_ref[(s, *lead)] = x_ref[:, s * width : (s + 1) * width].astype(out_ref.dtype)


def tiles(basis_ref):
    return [slice(start, start + TILE) for start in range(0, basis_ref.shape[0], TILE)]


def cut_kernel(x_ref, out_ref):
    spread(x_ref, out_ref)


def turn_kernel(x_ref, out_ref):
    out_ref[...] = x_ref[...].astype(f32).T.astype(bf16)


def right_kernel(a_ref, right_ref, out_ref, x_ref):
    for tile in tiles(right_ref):
        x_ref[:, tile] = jnp.dot(a_ref[...], right_ref[:, tile], preferred_element_type=f32)
    spread(x_ref, out_ref)


def moment_kernel(cols_ref, left_ref, out_ref):
    x = cols_ref[...].astype(f32).T.astype(bf16)
    for tile in tiles(left_ref):
        out_ref[:, tile] = jnp.dot(x, left_ref[:, tile], preferred_element_type=f32)


def middle_kernel(fix_ref, cols_ref, mom_ref, second_ref, left_ref, out_ref, rot_ref, dir_ref, back_ref):
    x = cols_ref[...].astype(f32).T.astype(bf16)
    for tile in tiles(left_ref):
        rot_grad = jnp.dot(x, left_ref[:, tile], preferred_element_type=f32)
        rot_ref[:, tile] = rot_grad
        rot_mom = beta_one * mom_ref[:, tile] + (1.0 - beta_one) * rot_grad
        second_new = beta_two * second_ref[:, tile].astype(f32) + (1.0 - beta_two) * rot_grad * rot_grad
        direction = rot_mom * fix_ref[0] / (jnp.sqrt(second_new * fix_ref[1]) + epsilon)
        dir_ref[:, tile] = direction.astype(bf16)
    spread(rot_ref, out_ref, 0)
    for tile in tiles(left_ref):
        back_ref[:, tile] = lax.dot_general(dir_ref[...], left_ref[tile, :], by_rows, preferred_element_type=f32)
    spread(back_ref, out_ref, 1)


def last_kernel(in_ref, second_ref, right_ref, second_out, update_out):
    columns = second_ref.shape[1]
    width = in_ref.shape[-1]
    rows = in_ref[:, 1].reshape(columns, width).astype(f32).T.astype(bf16)
    for tile in tiles(right_ref):
        update_out[:, tile] = lax.dot_general(rows, right_ref[tile, :], by_rows, preferred_element_type=f32).astype(bf16)
    rot_grad = in_ref[:, 0].reshape(columns, width).astype(f32).T
    second_out[...] = beta_two * second_ref[...] + (1.0 - beta_two) * rot_grad * rot_grad


def call(kernel, out_shape, in_specs, scratch, flops, moved):
    return pl.pallas_call(
        kernel,
        out_shape=out_shape,
        in_specs=in_specs,
        out_specs=jax.tree.map(lambda _: whole(), out_shape),
        scratch_shapes=scratch,
        compiler_params=pltpu.CompilerParams(vmem_limit_bytes=VMEM_LIMIT),
        cost_estimate=pl.CostEstimate(flops=flops, bytes_accessed=moved, transcendentals=0),
    )


def swap(pieces):
    return lax.all_to_all(pieces, "shard", split_axis=0, concat_axis=0, tiled=True)


def local(grad_parts, moment, second, left_basis, right_basis, block_steps):
    rows, columns = moment.shape[1:]
    product = 2 * rows * columns * columns
    basis_bytes = 2 * columns * columns
    narrow = pltpu.VMEM((rows, columns), bf16)
    wide = pltpu.VMEM((rows, columns), f32)
    pieces = jax.ShapeDtypeStruct((GROUP, rows, rows), bf16)
    turned = jax.ShapeDtypeStruct((rows, columns), bf16)
    summed = jax.ShapeDtypeStruct((rows, columns), f32)
    times_right = call(right_kernel, pieces, [whole(), whole()], [wide], product, basis_bytes)

    gradient = lax.psum_scatter(grad_parts[0], "dp", scatter_dimension=0, tiled=True)[0]
    right_full = lax.all_gather(right_basis[0], "shard", axis=0, tiled=True)
    left_full = lax.all_gather(left_basis[0], "shard", axis=0, tiled=True)
    second_cols = swap(call(cut_kernel, pieces, [whole()], [], 0, 6 * rows * columns)(second[0]))
    second_turned = call(turn_kernel, turned, [whole()], [], 0, 4 * rows * columns)(second_cols.reshape(columns, rows))
    mom_cols = swap(times_right(moment[0], right_full))
    gradient, second_turned, mom_cols = lax.optimization_barrier((gradient, second_turned, mom_cols))

    moment_new = (beta_one * moment[0].astype(f32) + (1.0 - beta_one) * gradient.astype(f32)).astype(bf16)
    grad_cols = swap(times_right(gradient, right_full))
    times_left = call(moment_kernel, summed, [whole()] * 2, [], product, basis_bytes)
    rot_mom_old = times_left(mom_cols.reshape(columns, rows), left_full)

    steps_float = block_steps[0].astype(f32)
    fixes = 1.0 / jnp.stack([1.0 - jnp.power(f32(beta_one), steps_float), 1.0 - jnp.power(f32(beta_two), steps_float)])
    both = jax.ShapeDtypeStruct((GROUP, 2, rows, rows), bf16)
    specs = [pl.BlockSpec(memory_space=pltpu.SMEM)] + [whole()] * 4
    middle = call(middle_kernel, both, specs, [wide, narrow, wide], 2 * product, basis_bytes)
    sent = middle(fixes, grad_cols.reshape(columns, rows), rot_mom_old, second_turned, left_full)

    got = swap(sent)
    last = call(last_kernel, (summed, turned), [whole()] * 3, [], product, basis_bytes)
    second_new, update = last(got, second[0], right_full)
    return (moment_new[None], second_new[None], update[None])


def solution(mesh):
    return jax.shard_map(
        local,
        mesh=mesh,
        in_specs=(
            P("dp", None, "shard", None),
            P("dp", "shard", None),
            P("dp", "shard", None),
            P("dp", "shard", None),
            P("dp", "shard", None),
            P("dp"),
        ),
        out_specs=(P("dp", "shard", None), P("dp", "shard", None), P("dp", "shard", None)),
        check_vma=False,
    )
```

```python
import jax
import jax.numpy as jnp
from jax import lax
from jax.experimental import pallas as pl
from jax.experimental.pallas import tpu as pltpu
from jax.sharding import PartitionSpec as P

beta_one = 0.8
beta_two = 0.95
epsilon = 1e-08
f32, bf16 = jnp.float32, jnp.bfloat16
GROUP = 16
TILE = 256
VMEM_LIMIT = 48 * 2**20
by_rows = (((1,), (1,)), ((), ()))


def whole():
    return pl.BlockSpec(memory_space=pltpu.VMEM)


def piece(x_ref, out_ref, s, lead=()):
    width = out_ref.shape[-1]
    out_ref[(s, *lead)] = x_ref[:, s * width : (s + 1) * width].astype(out_ref.dtype)


def ready(t, width):
    return range(t * TILE // width, (t + 1) * TILE // width)


def fetch(basis_ref, held, sems, by_column):
    copies = []
    for t in range(basis_ref.shape[0] // TILE):
        tile = pl.ds(t * TILE, TILE)
        spot = (slice(None), tile) if by_column else (tile, slice(None))
        copies.append(pltpu.make_async_copy(basis_ref.at[spot], held.at[spot], sems.at[t]))
        copies[-1].start()
    return copies


def cut_kernel(x_ref, out_ref):
    for s in range(GROUP):
        piece(x_ref, out_ref, s)


def turn_kernel(x_ref, out_ref):
    out_ref[...] = x_ref[...].astype(f32).T.astype(bf16)


def right_kernel(a_ref, right_ref, out_ref, x_ref, a_held, held, a_sem, sems, mix=lambda gradient: None):
    rows = pltpu.make_async_copy(a_ref, a_held, a_sem)
    rows.start()
    copies = fetch(right_ref, held, sems, True)
    rows.wait()
    mix(a_held)
    for t, copy in enumerate(copies):
        copy.wait()
        tile = slice(t * TILE, (t + 1) * TILE)
        x_ref[:, tile] = jnp.dot(a_held[...], held[:, tile], preferred_element_type=f32)
        for s in ready(t, out_ref.shape[-1]):
            piece(x_ref, out_ref, s)


def gradient_kernel(a_ref, right_ref, moment_ref, out_ref, moment_out, *scratch):
    def mix(gradient):
        new = beta_one * moment_ref[...].astype(f32) + (1.0 - beta_one) * gradient[...].astype(f32)
        moment_out[...] = new.astype(bf16)

    right_kernel(a_ref, right_ref, out_ref, *scratch, mix=mix)


def moment_kernel(cols_ref, left_ref, out_ref, held, sems):
    copies = fetch(left_ref, held, sems, True)
    x = cols_ref[...].astype(f32).T.astype(bf16)
    for t, copy in enumerate(copies):
        copy.wait()
        tile = slice(t * TILE, (t + 1) * TILE)
        out_ref[:, tile] = jnp.dot(x, held[:, tile], preferred_element_type=f32)


def middle_kernel(fix_ref, cols_ref, mom_ref, second_ref, left_ref, out_ref, rot_ref, dir_ref, back_ref, held, sems):
    copies = fetch(left_ref, held, sems, True)
    x = cols_ref[...].astype(f32).T.astype(bf16)
    for t, copy in enumerate(copies):
        copy.wait()
        tile = slice(t * TILE, (t + 1) * TILE)
        rot_grad = jnp.dot(x, held[:, tile], preferred_element_type=f32)
        rot_ref[:, tile] = rot_grad
        rot_mom = beta_one * mom_ref[:, tile] + (1.0 - beta_one) * rot_grad
        second_new = beta_two * second_ref[:, tile].astype(f32) + (1.0 - beta_two) * rot_grad * rot_grad
        direction = rot_mom * fix_ref[0] / (jnp.sqrt(second_new * fix_ref[1]) + epsilon)
        dir_ref[:, tile] = direction.astype(bf16)
        for s in ready(t, out_ref.shape[-1]):
            piece(rot_ref, out_ref, s, (0,))
    for t in range(len(copies)):
        tile = slice(t * TILE, (t + 1) * TILE)
        back_ref[:, tile] = lax.dot_general(dir_ref[...], held[tile, :], by_rows, preferred_element_type=f32)
        for s in ready(t, out_ref.shape[-1]):
            piece(back_ref, out_ref, s, (1,))


def last_kernel(in_ref, second_ref, right_ref, second_out, update_out, held, sems):
    copies = fetch(right_ref, held, sems, False)
    columns = second_ref.shape[1]
    width = in_ref.shape[-1]
    rows = in_ref[:, 1].reshape(columns, width).astype(f32).T.astype(bf16)
    rot_grad = in_ref[:, 0].reshape(columns, width).astype(f32).T
    second_out[...] = beta_two * second_ref[...] + (1.0 - beta_two) * rot_grad * rot_grad
    for t, copy in enumerate(copies):
        copy.wait()
        tile = slice(t * TILE, (t + 1) * TILE)
        update_out[:, tile] = lax.dot_general(rows, held[tile, :], by_rows, preferred_element_type=f32).astype(bf16)


def call(kernel, out_shape, in_specs, scratch, flops, moved):
    return pl.pallas_call(
        kernel,
        out_shape=out_shape,
        in_specs=in_specs,
        out_specs=jax.tree.map(lambda _: whole(), out_shape),
        scratch_shapes=scratch,
        compiler_params=pltpu.CompilerParams(vmem_limit_bytes=VMEM_LIMIT),
        cost_estimate=pl.CostEstimate(flops=flops, bytes_accessed=moved, transcendentals=0),
    )


def swap(pieces):
    return lax.all_to_all(pieces, "shard", split_axis=0, concat_axis=0, tiled=True)


def local(grad_parts, moment, second, left_basis, right_basis, block_steps):
    rows, columns = moment.shape[1:]
    product = 2 * rows * columns * columns
    basis_bytes = 2 * columns * columns
    apart = pl.BlockSpec(memory_space=pltpu.HBM)
    narrow = pltpu.VMEM((rows, columns), bf16)
    wide = pltpu.VMEM((rows, columns), f32)
    basis = [pltpu.VMEM((columns, columns), bf16), pltpu.SemaphoreType.DMA((columns // TILE,))]
    pieces = jax.ShapeDtypeStruct((GROUP, rows, rows), bf16)
    turned = jax.ShapeDtypeStruct((rows, columns), bf16)
    summed = jax.ShapeDtypeStruct((rows, columns), f32)
    right_scratch = [wide, narrow, basis[0], pltpu.SemaphoreType.DMA, basis[1]]

    gradient = lax.psum_scatter(grad_parts[0], "dp", scatter_dimension=0, tiled=True)[0]
    right_full = lax.all_gather(right_basis[0], "shard", axis=0, tiled=True)
    left_full = lax.all_gather(left_basis[0], "shard", axis=0, tiled=True)
    second_cols = swap(call(cut_kernel, pieces, [whole()], [], 0, 6 * rows * columns)(second[0]))
    second_turned = call(turn_kernel, turned, [whole()], [], 0, 4 * rows * columns)(second_cols.reshape(columns, rows))
    times_right = call(right_kernel, pieces, [apart, apart], right_scratch, product, basis_bytes)
    mom_cols = swap(times_right(moment[0], right_full))
    gradient, second_turned, mom_cols = lax.optimization_barrier((gradient, second_turned, mom_cols))

    times_right = call(gradient_kernel, (pieces, turned), [apart, apart, whole()], right_scratch, product, basis_bytes)
    grad_right, moment_new = times_right(gradient, right_full, moment[0])
    grad_cols = swap(grad_right)
    times_left = call(moment_kernel, summed, [whole(), apart], basis, product, basis_bytes)
    rot_mom_old = times_left(mom_cols.reshape(columns, rows), left_full)

    steps_float = block_steps[0].astype(f32)
    fixes = 1.0 / jnp.stack([1.0 - jnp.power(f32(beta_one), steps_float), 1.0 - jnp.power(f32(beta_two), steps_float)])
    both = jax.ShapeDtypeStruct((GROUP, 2, rows, rows), bf16)
    specs = [pl.BlockSpec(memory_space=pltpu.SMEM), whole(), whole(), whole(), apart]
    middle = call(middle_kernel, both, specs, [wide, narrow, wide, *basis], 2 * product, basis_bytes)
    sent = middle(fixes, grad_cols.reshape(columns, rows), rot_mom_old, second_turned, left_full)

    got = swap(sent)
    last = call(last_kernel, (summed, turned), [whole(), whole(), apart], basis, product, basis_bytes)
    second_new, update = last(got, second[0], right_full)
    return (moment_new[None], second_new[None], update[None])


def solution(mesh):
    return jax.shard_map(
        local,
        mesh=mesh,
        in_specs=(
            P("dp", None, "shard", None),
            P("dp", "shard", None),
            P("dp", "shard", None),
            P("dp", "shard", None),
            P("dp", "shard", None),
            P("dp"),
        ),
        out_specs=(P("dp", "shard", None), P("dp", "shard", None), P("dp", "shard", None)),
        check_vma=False,
    )
```

```python
import jax
import jax.numpy as jnp
from jax import lax
from jax.experimental import pallas as pl
from jax.experimental.pallas import tpu as pltpu
from jax.sharding import PartitionSpec as P

beta_one = 0.8
beta_two = 0.95
epsilon = 1e-08
f32, bf16 = jnp.float32, jnp.bfloat16
GROUP = 16
TILE = 256
VMEM_LIMIT = 48 * 2**20
by_rows = (((1,), (1,)), ((), ()))


def whole():
    return pl.BlockSpec(memory_space=pltpu.VMEM)


def piece(x_ref, out_ref, s, lead=()):
    width = out_ref.shape[-1]
    out_ref[(s, *lead)] = x_ref[:, s * width : (s + 1) * width].astype(out_ref.dtype)


def fetch(basis_ref, held, sems):
    copies = []
    for t in range(basis_ref.shape[0] // TILE):
        tile = pl.ds(t * TILE, TILE)
        copies.append(pltpu.make_async_copy(basis_ref.at[tile, :], held.at[tile, :], sems.at[t]))
        copies[-1].start()
    return copies


def product_into(out_ref, x_ref, copies, held):
    for t, copy in enumerate(copies):
        copy.wait()
        tile = slice(t * TILE, (t + 1) * TILE)
        part = jnp.dot(x_ref[:, tile], held[tile, :], preferred_element_type=f32)
        out_ref[...] = part if t == 0 else out_ref[...] + part


def cut_kernel(x_ref, out_ref):
    for s in range(GROUP):
        piece(x_ref, out_ref, s)


def turn_kernel(x_ref, out_ref):
    out_ref[...] = x_ref[...].astype(f32).T.astype(bf16)


def right_kernel(a_ref, right_ref, out_ref, x_ref, a_held, held, a_sem, sems, mix=lambda gradient: None):
    rows = pltpu.make_async_copy(a_ref, a_held, a_sem)
    rows.start()
    copies = fetch(right_ref, held, sems)
    rows.wait()
    mix(a_held)
    product_into(x_ref, a_held, copies, held)
    for s in range(GROUP):
        piece(x_ref, out_ref, s)


def gradient_kernel(a_ref, right_ref, moment_ref, out_ref, moment_out, *scratch):
    def mix(gradient):
        new = beta_one * moment_ref[...].astype(f32) + (1.0 - beta_one) * gradient[...].astype(f32)
        moment_out[...] = new.astype(bf16)

    right_kernel(a_ref, right_ref, out_ref, *scratch, mix=mix)


def moment_kernel(cols_ref, left_ref, out_ref, x_ref, held, sems):
    copies = fetch(left_ref, held, sems)
    x_ref[...] = cols_ref[...].astype(f32).T.astype(bf16)
    product_into(out_ref, x_ref, copies, held)


def middle_kernel(fix_ref, cols_ref, mom_ref, second_ref, left_ref, out_ref, rot_ref, x_ref, back_ref, held, sems):
    copies = fetch(left_ref, held, sems)
    x_ref[...] = cols_ref[...].astype(f32).T.astype(bf16)
    product_into(rot_ref, x_ref, copies, held)
    rot_grad = rot_ref[...]
    rot_mom = beta_one * mom_ref[...] + (1.0 - beta_one) * rot_grad
    second_new = beta_two * second_ref[...].astype(f32) + (1.0 - beta_two) * rot_grad * rot_grad
    direction = rot_mom * fix_ref[0] / (jnp.sqrt(second_new * fix_ref[1]) + epsilon)
    x_ref[...] = direction.astype(bf16)
    for t in range(len(copies)):
        tile = slice(t * TILE, (t + 1) * TILE)
        back_ref[:, tile] = lax.dot_general(x_ref[...], held[tile, :], by_rows, preferred_element_type=f32)
    for s in range(GROUP):
        piece(rot_ref, out_ref, s, (0,))
        piece(back_ref, out_ref, s, (1,))


def last_kernel(in_ref, second_ref, right_ref, second_out, update_out, held, sems):
    copies = fetch(right_ref, held, sems)
    columns = second_ref.shape[1]
    width = in_ref.shape[-1]
    rows = in_ref[:, 1].reshape(columns, width).astype(f32).T.astype(bf16)
    rot_grad = in_ref[:, 0].reshape(columns, width).astype(f32).T
    second_out[...] = beta_two * second_ref[...] + (1.0 - beta_two) * rot_grad * rot_grad
    for t, copy in enumerate(copies):
        copy.wait()
        tile = slice(t * TILE, (t + 1) * TILE)
        update_out[:, tile] = lax.dot_general(rows, held[tile, :], by_rows, preferred_element_type=f32).astype(bf16)


def call(kernel, out_shape, in_specs, scratch, flops, moved):
    return pl.pallas_call(
        kernel,
        out_shape=out_shape,
        in_specs=in_specs,
        out_specs=jax.tree.map(lambda _: whole(), out_shape),
        scratch_shapes=scratch,
        compiler_params=pltpu.CompilerParams(vmem_limit_bytes=VMEM_LIMIT),
        cost_estimate=pl.CostEstimate(flops=flops, bytes_accessed=moved, transcendentals=0),
    )


def swap(pieces):
    return lax.all_to_all(pieces, "shard", split_axis=0, concat_axis=0, tiled=True)


def local(grad_parts, moment, second, left_basis, right_basis, block_steps):
    rows, columns = moment.shape[1:]
    product = 2 * rows * columns * columns
    basis_bytes = 2 * columns * columns
    apart = pl.BlockSpec(memory_space=pltpu.HBM)
    narrow = pltpu.VMEM((rows, columns), bf16)
    wide = pltpu.VMEM((rows, columns), f32)
    basis = [pltpu.VMEM((columns, columns), bf16), pltpu.SemaphoreType.DMA((columns // TILE,))]
    pieces = jax.ShapeDtypeStruct((GROUP, rows, rows), bf16)
    turned = jax.ShapeDtypeStruct((rows, columns), bf16)
    summed = jax.ShapeDtypeStruct((rows, columns), f32)
    right_scratch = [wide, narrow, basis[0], pltpu.SemaphoreType.DMA, basis[1]]

    gradient = lax.psum_scatter(grad_parts[0], "dp", scatter_dimension=0, tiled=True)[0]
    right_full = lax.all_gather(right_basis[0], "shard", axis=0, tiled=True)
    left_full = lax.all_gather(left_basis[0], "shard", axis=0, tiled=True)
    second_cols = swap(call(cut_kernel, pieces, [whole()], [], 0, 6 * rows * columns)(second[0]))
    second_turned = call(turn_kernel, turned, [whole()], [], 0, 4 * rows * columns)(second_cols.reshape(columns, rows))
    times_right = call(right_kernel, pieces, [apart, apart], right_scratch, product, basis_bytes)
    mom_cols = swap(times_right(moment[0], right_full))
    gradient, second_turned, mom_cols = lax.optimization_barrier((gradient, second_turned, mom_cols))

    times_right = call(gradient_kernel, (pieces, turned), [apart, apart, whole()], right_scratch, product, basis_bytes)
    grad_right, moment_new = times_right(gradient, right_full, moment[0])
    grad_cols = swap(grad_right)
    times_left = call(moment_kernel, summed, [whole(), apart], [narrow, *basis], product, basis_bytes)
    rot_mom_old = times_left(mom_cols.reshape(columns, rows), left_full)

    steps_float = block_steps[0].astype(f32)
    fixes = 1.0 / jnp.stack([1.0 - jnp.power(f32(beta_one), steps_float), 1.0 - jnp.power(f32(beta_two), steps_float)])
    both = jax.ShapeDtypeStruct((GROUP, 2, rows, rows), bf16)
    specs = [pl.BlockSpec(memory_space=pltpu.SMEM), whole(), whole(), whole(), apart]
    middle = call(middle_kernel, both, specs, [wide, narrow, wide, *basis], 2 * product, basis_bytes)
    sent = middle(fixes, grad_cols.reshape(columns, rows), rot_mom_old, second_turned, left_full)

    got = swap(sent)
    last = call(last_kernel, (summed, turned), [whole(), whole(), apart], basis, product, basis_bytes)
    second_new, update = last(got, second[0], right_full)
    return (moment_new[None], second_new[None], update[None])


def solution(mesh):
    return jax.shard_map(
        local,
        mesh=mesh,
        in_specs=(
            P("dp", None, "shard", None),
            P("dp", "shard", None),
            P("dp", "shard", None),
            P("dp", "shard", None),
            P("dp", "shard", None),
            P("dp"),
        ),
        out_specs=(P("dp", "shard", None), P("dp", "shard", None), P("dp", "shard", None)),
        check_vma=False,
    )
```

```python
import jax
import jax.numpy as jnp
from jax import lax
from jax.experimental import pallas as pl
from jax.experimental.pallas import tpu as pltpu
from jax.sharding import PartitionSpec as P

beta_one = 0.8
beta_two = 0.95
epsilon = 1e-08
f32, bf16 = jnp.float32, jnp.bfloat16
GROUP = 16
TILE = 256
VMEM_LIMIT = 48 * 2**20
by_rows = (((1,), (1,)), ((), ()))


def whole():
    return pl.BlockSpec(memory_space=pltpu.VMEM)


def piece(x_ref, out_ref, s, lead=()):
    width = out_ref.shape[-1]
    out_ref[(s, *lead)] = x_ref[:, s * width : (s + 1) * width].astype(out_ref.dtype)


def fetch(basis_ref, held, sems):
    copies = []
    for t in range(basis_ref.shape[0] // TILE):
        tile = pl.ds(t * TILE, TILE)
        copies.append(pltpu.make_async_copy(basis_ref.at[tile, :], held.at[tile, :], sems.at[t]))
        copies[-1].start()
    return copies


def product_into(out_ref, x_ref, copies, held):
    for t, copy in enumerate(copies):
        copy.wait()
        tile = slice(t * TILE, (t + 1) * TILE)
        part = jnp.dot(x_ref[:, tile], held[tile, :], preferred_element_type=f32)
        out_ref[...] = part if t == 0 else out_ref[...] + part


def cut_kernel(x_ref, out_ref):
    for s in range(GROUP):
        piece(x_ref, out_ref, s)


def turn_kernel(x_ref, out_ref):
    out_ref[...] = x_ref[...].T


def right_kernel(a_ref, right_ref, out_ref, x_ref, a_held, held, a_sem, sems, mix=lambda gradient: None):
    rows = pltpu.make_async_copy(a_ref, a_held, a_sem)
    rows.start()
    copies = fetch(right_ref, held, sems)
    rows.wait()
    mix(a_held)
    product_into(x_ref, a_held, copies, held)
    for s in range(GROUP):
        piece(x_ref, out_ref, s)


def gradient_kernel(a_ref, right_ref, moment_ref, out_ref, moment_out, *scratch):
    def mix(gradient):
        new = beta_one * moment_ref[...].astype(f32) + (1.0 - beta_one) * gradient[...].astype(f32)
        moment_out[...] = new.astype(bf16)

    right_kernel(a_ref, right_ref, out_ref, *scratch, mix=mix)


def moment_kernel(cols_ref, left_ref, out_ref, x_ref, held, sems):
    copies = fetch(left_ref, held, sems)
    x_ref[...] = cols_ref[...].T
    product_into(out_ref, x_ref, copies, held)


def middle_kernel(fix_ref, cols_ref, mom_ref, second_ref, left_ref, out_ref, rot_ref, x_ref, back_ref, held, sems):
    copies = fetch(left_ref, held, sems)
    x_ref[...] = cols_ref[...].T
    product_into(rot_ref, x_ref, copies, held)
    rot_grad = rot_ref[...]
    rot_mom = beta_one * mom_ref[...] + (1.0 - beta_one) * rot_grad
    second_new = beta_two * second_ref[...].astype(f32) + (1.0 - beta_two) * rot_grad * rot_grad
    direction = rot_mom * fix_ref[0] / (jnp.sqrt(second_new * fix_ref[1]) + epsilon)
    x_ref[...] = direction.astype(bf16)
    for t in range(len(copies)):
        tile = slice(t * TILE, (t + 1) * TILE)
        back_ref[:, tile] = lax.dot_general(x_ref[...], held[tile, :], by_rows, preferred_element_type=f32)
    for s in range(GROUP):
        piece(rot_ref, out_ref, s, (0,))
        piece(back_ref, out_ref, s, (1,))


def last_kernel(in_ref, second_ref, right_ref, second_out, update_out, held, sems):
    copies = fetch(right_ref, held, sems)
    columns = second_ref.shape[1]
    width = in_ref.shape[-1]
    rows = in_ref[:, 1].reshape(columns, width).T
    rot_grad = in_ref[:, 0].reshape(columns, width).T.astype(f32)
    second_out[...] = beta_two * second_ref[...] + (1.0 - beta_two) * rot_grad * rot_grad
    for t, copy in enumerate(copies):
        copy.wait()
        tile = slice(t * TILE, (t + 1) * TILE)
        update_out[:, tile] = lax.dot_general(rows, held[tile, :], by_rows, preferred_element_type=f32).astype(bf16)


def call(kernel, out_shape, in_specs, scratch, flops, moved):
    return pl.pallas_call(
        kernel,
        out_shape=out_shape,
        in_specs=in_specs,
        out_specs=jax.tree.map(lambda _: whole(), out_shape),
        scratch_shapes=scratch,
        compiler_params=pltpu.CompilerParams(vmem_limit_bytes=VMEM_LIMIT),
        cost_estimate=pl.CostEstimate(flops=flops, bytes_accessed=moved, transcendentals=0),
    )


def swap(pieces):
    return lax.all_to_all(pieces, "shard", split_axis=0, concat_axis=0, tiled=True)


def local(grad_parts, moment, second, left_basis, right_basis, block_steps):
    rows, columns = moment.shape[1:]
    product = 2 * rows * columns * columns
    basis_bytes = 2 * columns * columns
    apart = pl.BlockSpec(memory_space=pltpu.HBM)
    narrow = pltpu.VMEM((rows, columns), bf16)
    wide = pltpu.VMEM((rows, columns), f32)
    basis = [pltpu.VMEM((columns, columns), bf16), pltpu.SemaphoreType.DMA((columns // TILE,))]
    pieces = jax.ShapeDtypeStruct((GROUP, rows, rows), bf16)
    turned = jax.ShapeDtypeStruct((rows, columns), bf16)
    summed = jax.ShapeDtypeStruct((rows, columns), f32)
    right_scratch = [wide, narrow, basis[0], pltpu.SemaphoreType.DMA, basis[1]]

    gradient = lax.psum_scatter(grad_parts[0], "dp", scatter_dimension=0, tiled=True)[0]
    right_full = lax.all_gather(right_basis[0], "shard", axis=0, tiled=True)
    left_full = lax.all_gather(left_basis[0], "shard", axis=0, tiled=True)
    second_cols = swap(call(cut_kernel, pieces, [whole()], [], 0, 6 * rows * columns)(second[0]))
    second_turned = call(turn_kernel, turned, [whole()], [], 0, 4 * rows * columns)(second_cols.reshape(columns, rows))
    times_right = call(right_kernel, pieces, [apart, apart], right_scratch, product, basis_bytes)
    mom_cols = swap(times_right(moment[0], right_full))
    gradient, second_turned, mom_cols = lax.optimization_barrier((gradient, second_turned, mom_cols))

    times_right = call(gradient_kernel, (pieces, turned), [apart, apart, whole()], right_scratch, product, basis_bytes)
    grad_right, moment_new = times_right(gradient, right_full, moment[0])
    grad_cols = swap(grad_right)
    times_left = call(moment_kernel, summed, [whole(), apart], [narrow, *basis], product, basis_bytes)
    rot_mom_old = times_left(mom_cols.reshape(columns, rows), left_full)

    steps_float = block_steps[0].astype(f32)
    fixes = 1.0 / jnp.stack([1.0 - jnp.power(f32(beta_one), steps_float), 1.0 - jnp.power(f32(beta_two), steps_float)])
    both = jax.ShapeDtypeStruct((GROUP, 2, rows, rows), bf16)
    specs = [pl.BlockSpec(memory_space=pltpu.SMEM), whole(), whole(), whole(), apart]
    middle = call(middle_kernel, both, specs, [wide, narrow, wide, *basis], 2 * product, basis_bytes)
    sent = middle(fixes, grad_cols.reshape(columns, rows), rot_mom_old, second_turned, left_full)

    got = swap(sent)
    last = call(last_kernel, (summed, turned), [whole(), whole(), apart], basis, product, basis_bytes)
    second_new, update = last(got, second[0], right_full)
    return (moment_new[None], second_new[None], update[None])


def solution(mesh):
    return jax.shard_map(
        local,
        mesh=mesh,
        in_specs=(
            P("dp", None, "shard", None),
            P("dp", "shard", None),
            P("dp", "shard", None),
            P("dp", "shard", None),
            P("dp", "shard", None),
            P("dp"),
        ),
        out_specs=(P("dp", "shard", None), P("dp", "shard", None), P("dp", "shard", None)),
        check_vma=False,
    )
```
